32 devices in a mesh: grp: 2 (over x), node: 16 (over z, y, core).
Axes of the slice: x: 2, y: 2, z: 4, core: 2. Of those that a mesh axis runs over, the one named last changes fastest.
Arguments:
- grid_inputs: bfloat16 [32768, 474], P(('grp', 'node')), parts along dimension 0, may hold values from -6 to 6
- mesh_latent: bfloat16 [512, 512], P(('grp', 'node')), parts along dimension 0, may hold values from -6 to 6
- sender_ids: int32 [65536], P(('grp', 'node')), parts along dimension 0, may hold values from 0 to 1023
- receiver_ids: int32 [65536], P(('grp', 'node')), parts along dimension 0, may hold values from 0 to 255
- embed_weight: bfloat16 [474, 512], replicated, may hold values from -0.25 to 0.25
- sender_weight: bfloat16 [512, 512], replicated, may hold values from -0.25 to 0.25
- receiver_weight: bfloat16 [512, 512], replicated, may hold values from -0.25 to 0.25
- message_weight: bfloat16 [512, 512], replicated, may hold values from -0.25 to 0.25
- norm_gain: float32 [512], replicated, may hold values from 0.25 to 1.75
- out_grad: bfloat16 [512, 512], P(('grp', 'node')), parts along dimension 0, may hold values from -6 to 6
Outputs:
- mesh_update: bfloat16 [512, 512], P(('grp', 'node')), parts along dimension 0
- mesh_grad: bfloat16 [512, 512], P(('grp', 'node')), parts along dimension 0
- message_grad: float32 [1024, 512], P('grp'), parts along dimension 0
The draws below stay inside these ranges and needn't reach their ends.
There are 2 independent parts, one for each index of `grp`. The reference program is written for one: setup_inputs(seed, part) draws one part's arguments, and reference() takes and returns one part's arrays. A program takes and returns all parts, laid end to end along the dimension named above; an argument that names none is the same for every part. Nothing has to cross between parts.
All inputs are finite; a program needn't handle non-finite values.
Results may differ from the reference program's by a relative error of at most 0.0052.
Values may be sent and summed in bfloat16 or wider, within the bound.
A program may use at most 64 MiB of HBM per device.

```python
import math
import jax
import jax.numpy as jnp
from jax import lax

L = 512
C_IN = 474
G_DEV = 1024
EB = 16
BLK = 128
GRID = 16384
MESH = 256
EDGES = 32768
N_NODE = 16


def set_ends(entries, key, low, high):
    place = [jax.random.randint(jax.random.fold_in(key, axis), (), 0, length) for axis, length in enumerate(entries.shape)]
    main_axis = entries.shape.index(max(entries.shape))
    next_to = place[:main_axis] + [(place[main_axis] + 1) % entries.shape[main_axis]] + place[main_axis + 1:]
    return entries.at[tuple(place)].set(low).at[tuple(next_to)].set(high)


def levels(key, dims, shards, smallest, high):
    loudness, own = 1.0, jax.random.fold_in(key, 6)
    for dim, shards_of in shards:
        steps = jnp.exp(jax.random.uniform(jax.random.fold_in(own, dim), (shards_of,), jnp.float32, smallest / len(shards), high / len(shards)))
        loudness = loudness * jnp.repeat(steps, dims[dim] // shards_of).reshape([-1 if axis == dim else 1 for axis in range(len(dims))])
    return loudness


def gaussian(rng, dims, width, limit, pieces=(), kind=jnp.bfloat16):
    gain = levels(rng, dims, pieces, -0.22, 0.18) if pieces else 1.0
    array = jax.random.normal(rng, dims, jnp.float32) * width * gain
    return jnp.minimum(jnp.maximum(array, -limit), limit).astype(kind)


def setup_inputs(seed: int = 0, part: int = 0) -> dict:
    splits = jax.random.split(jax.random.key(seed), 11)
    part_keys = jax.random.split(jax.random.fold_in(splits[10], part), 11)
    return {
        "grid_inputs": gaussian(part_keys[0], (GRID, C_IN), 1.0, 6.0, ((0, 16),)),
        "mesh_latent": gaussian(part_keys[1], (MESH, L), 1.0, 6.0, ((0, 16),)),
        "sender_ids": set_ends(jax.random.randint(part_keys[2], (EDGES,), 0, G_DEV), jax.random.fold_in(part_keys[2], 1), 0, G_DEV - 1).astype(jnp.int32),
        "receiver_ids": set_ends(jax.random.randint(part_keys[3], (EDGES,), 0, MESH), jax.random.fold_in(part_keys[3], 1), 0, MESH - 1).astype(jnp.int32),
        "embed_weight": gaussian(splits[4], (C_IN, L), C_IN ** -0.5, 0.25),
        "sender_weight": gaussian(splits[5], (L, L), L ** -0.5, 0.25),
        "receiver_weight": gaussian(splits[6], (L, L), L ** -0.5, 0.25),
        "message_weight": gaussian(splits[7], (L, L), L ** -0.5, 0.25),
        "norm_gain": jnp.clip(1.0 + 0.15 * jax.random.normal(splits[8], (L,), jnp.float32), 0.25, 1.75),
        "out_grad": gaussian(part_keys[9], (MESH, L), 1.0, 6.0, ((0, 16),)),
    }


def reference(grid_inputs, mesh_latent, sender_ids, receiver_ids, embed_weight, sender_weight, receiver_weight, message_weight, norm_gain, out_grad):
    grid_latent = jax.nn.silu(jnp.dot(grid_inputs, embed_weight, preferred_element_type=jnp.float32)).astype(jnp.bfloat16)
    send_term = jnp.dot(grid_latent, sender_weight, preferred_element_type=jnp.float32)
    recv_term = jnp.dot(mesh_latent, receiver_weight, preferred_element_type=jnp.float32).astype(jnp.bfloat16)
    edge_index = jnp.arange(EDGES, dtype=jnp.int32)
    senders = (edge_index // (EB * BLK) * G_DEV + sender_ids).astype(jnp.int32)
    sender_blocks = senders.reshape(N_NODE, EB * BLK)
    receiver_blocks = receiver_ids.reshape(N_NODE, EB * BLK)

    def forward_step(running, pair):
        senders_here, receivers_here = pair
        preact = send_term[senders_here] + recv_term[receivers_here].astype(send_term.dtype)
        hidden = jax.nn.silu(preact).astype(jnp.bfloat16)
        message = jnp.dot(hidden, message_weight, preferred_element_type=jnp.float32)
        return (running + jax.ops.segment_sum(message, receivers_here, num_segments=MESH), None)
    summed, _ = lax.scan(forward_step, jnp.zeros((MESH, L), send_term.dtype), (sender_blocks, receiver_blocks))
    inverse = lax.rsqrt(lax.optimization_barrier(jnp.mean(summed * summed, axis=-1, keepdims=True)) + 1e-05)
    normed = summed * inverse
    mesh_update = (mesh_latent.astype(summed.dtype) + normed * norm_gain).astype(jnp.bfloat16)
    upstream = out_grad.astype(summed.dtype)
    dnorm = upstream * norm_gain
    agg_grad = (inverse * (dnorm - normed * lax.optimization_barrier(jnp.mean(dnorm * normed, axis=-1, keepdims=True)))).astype(jnp.bfloat16)

    def backward_step(running, pair):
        weight_total, recv_total = running
        senders_here, receivers_here = pair
        preact = send_term[senders_here] + recv_term[receivers_here].astype(send_term.dtype)
        hidden = jax.nn.silu(preact).astype(jnp.bfloat16)
        edge_grad = agg_grad[receivers_here]
        weight_total = weight_total + jnp.dot(hidden.T, edge_grad, preferred_element_type=jnp.float32)
        hidden_grad = jnp.dot(edge_grad, message_weight.T, preferred_element_type=jnp.float32)
        gates = jax.nn.sigmoid(preact)
        preact_grad = hidden_grad * gates * (1.0 + preact * (1.0 - gates))
        recv_total = recv_total + jax.ops.segment_sum(preact_grad, receivers_here, num_segments=MESH)
        return ((weight_total, recv_total), None)
    start = (jnp.zeros((L, L), send_term.dtype), jnp.zeros((MESH, L), send_term.dtype))
    (weight_total, recv_total), _ = lax.scan(backward_step, start, (sender_blocks, receiver_blocks))
    message_grad = weight_total / math.sqrt(EDGES)
    recv_grad = recv_total.astype(jnp.bfloat16)
    mesh_grad = (upstream + jnp.dot(recv_grad, receiver_weight.T, preferred_element_type=jnp.float32)).astype(jnp.bfloat16)
    return (mesh_update, mesh_grad, message_grad)
```

```python
import math

import jax
import jax.numpy as jnp
from jax import lax
from jax.sharding import PartitionSpec as P


def shards(
    grid_inputs,
    mesh_latent,
    sender_ids,
    receiver_ids,
    embed_weight,
    sender_weight,
    receiver_weight,
    message_weight,
    norm_gain,
    out_grad,
):
    n = lax.axis_size("node")
    owned = mesh_latent.shape[0]
    me = lax.axis_index("node")
    gathered = lax.all_gather(jnp.concatenate([mesh_latent, out_grad], axis=1), "node", axis=0, tiled=True)
    width = mesh_latent.shape[1]
    all_latent, all_grad = gathered[:, :width], gathered[:, width:]
    grid_latent = jax.nn.silu(
        jnp.dot(grid_inputs, embed_weight, preferred_element_type=jnp.float32)
    ).astype(jnp.bfloat16)
    send_term = jnp.dot(grid_latent, sender_weight, preferred_element_type=jnp.float32).astype(jnp.bfloat16)
    recv_term = jnp.dot(all_latent, receiver_weight, preferred_element_type=jnp.float32).astype(jnp.bfloat16)
    nodes = jnp.arange(owned * n, dtype=jnp.int32)
    by_sender = (sender_ids[:, None] == jnp.arange(grid_inputs.shape[0], dtype=jnp.int32)[None, :]).astype(jnp.bfloat16)
    by_receiver = (receiver_ids[:, None] == nodes[None, :]).astype(jnp.bfloat16)
    to_receiver = (nodes[:, None] == receiver_ids[None, :]).astype(jnp.bfloat16)
    preact = jnp.dot(by_sender, send_term, preferred_element_type=jnp.float32) + jnp.dot(
        by_receiver, recv_term, preferred_element_type=jnp.float32
    )
    gates = jax.nn.sigmoid(preact)
    hidden = (preact * gates).astype(jnp.bfloat16)
    slope = (gates * (1.0 + preact * (1.0 - gates))).astype(jnp.bfloat16)
    part = jnp.dot(to_receiver, jnp.concatenate([hidden, slope], axis=1), preferred_element_type=jnp.float32)
    both = lax.psum_scatter(part, "node", scatter_dimension=0, tiled=True)
    own_slope = both[:, width:]
    hidden_sum = lax.all_gather(both[:, :width].astype(jnp.bfloat16), "node", axis=0, tiled=True)
    summed = jnp.dot(hidden_sum, message_weight, preferred_element_type=jnp.float32)
    inverse = lax.rsqrt(jnp.mean(summed * summed, axis=-1, keepdims=True) + 1e-05)
    normed = summed * inverse
    upstream = all_grad.astype(jnp.float32)
    dnorm = upstream * norm_gain
    agg_grad = (
        inverse * (dnorm - normed * jnp.mean(dnorm * normed, axis=-1, keepdims=True))
    ).astype(jnp.bfloat16)
    own_normed = lax.dynamic_slice_in_dim(normed, me * owned, owned, 0)
    own_agg = lax.dynamic_slice_in_dim(agg_grad, me * owned, owned, 0)
    mesh_update = (mesh_latent.astype(jnp.float32) + own_normed * norm_gain).astype(jnp.bfloat16)
    hidden_grad = lax.dot_general(
        own_agg, message_weight, (((1,), (1,)), ((), ())), preferred_element_type=jnp.float32
    )
    recv_grad = (hidden_grad * own_slope).astype(jnp.bfloat16)
    mesh_grad = (
        out_grad.astype(jnp.float32)
        + lax.dot_general(
            recv_grad, receiver_weight, (((1,), (1,)), ((), ())), preferred_element_type=jnp.float32
        )
    ).astype(jnp.bfloat16)
    edge_total = receiver_ids.shape[0] * n
    message_grad = lax.dot_general(
        hidden_sum, agg_grad, (((0,), (0,)), ((), ())), preferred_element_type=jnp.float32
    ) / math.sqrt(edge_total)
    return (mesh_update, mesh_grad, message_grad)


def solution(mesh):
    placed = (
        P(("grp", "node"), None),
        P(("grp", "node"), None),
        P(("grp", "node")),
        P(("grp", "node")),
        P(),
        P(),
        P(),
        P(),
        P(),
        P(("grp", "node"), None),
    )
    return jax.shard_map(
        shards,
        mesh=mesh,
        in_specs=placed,
        out_specs=(P(("grp", "node"), None), P(("grp", "node"), None), P("grp", None)),
        check_vma=False,
    )
```

```python
import functools
import math

import jax
import jax.numpy as jnp
from jax import lax
from jax.experimental import pallas as pl
from jax.experimental.pallas import tpu as pltpu
from jax.sharding import PartitionSpec as P

LOGICAL = pl.DeviceIdType.MESH
F32 = jnp.float32
BF16 = jnp.bfloat16
CHUNK = 512
LANES = 128


def dot_nn(a, b):
    return jnp.dot(a, b, preferred_element_type=F32)


def dot_nt(a, b):
    return lax.dot_general(a, b, (((1,), (1,)), ((), ())), preferred_element_type=F32)


def dot_tn(a, b):
    return lax.dot_general(a, b, (((0,), (0,)), ((), ())), preferred_element_type=F32)


def selector(ids_row, columns):
    column = jnp.broadcast_to(ids_row, (LANES, LANES)).T
    lane = lax.broadcasted_iota(jnp.int32, (LANES, LANES), 1)
    parts = [
        jnp.where(column == lane + start, 1.0, 0.0).astype(BF16)
        for start in range(0, columns, LANES)
    ]
    return jnp.concatenate(parts, axis=1)


def kernel(
    chips,
    edge_total,
    grid_ref,
    latent_ref,
    sender_ref,
    receiver_ref,
    embed_ref,
    sendw_ref,
    recvw_ref,
    messw_ref,
    gain_ref,
    grad_ref,
    update_ref,
    meshgrad_ref,
    weight_ref,
    latents,
    grads,
    hsums,
    table,
    rtable,
    picked,
    picks,
    rpicks,
    acc,
    outgoing,
    pair_in,
    chip_sum,
    peer_in,
    send_ici,
    recv_ici,
    send_core,
    recv_core,
    pair_send,
    pair_recv,
    peer_send,
    peer_recv,
):
    grp = lax.axis_index("grp")
    me = lax.axis_index("node")
    chip = me // 2
    core = me % 2
    other = 1 - core
    partner = (grp, chip * 2 + other)
    owned, width = latent_ref.shape
    half = chips * owned
    nodes = 2 * half
    sub_rows = sender_ref.shape[0]
    shift = owned.bit_length() - 1

    def peer(k):
        return lax.rem(chip + k, chips)

    barrier = pltpu.get_barrier_semaphore()

    def greet(k, carry):
        pl.semaphore_signal(barrier, inc=1, device_id=(grp, peer(k) * 2 + core), device_id_type=LOGICAL)
        return carry

    lax.fori_loop(1, chips, greet, 0)
    pl.semaphore_signal(barrier, inc=1, device_id=partner, device_id_type=LOGICAL)
    latents[core, chip] = latent_ref[...]
    grads[core, chip] = grad_ref[...]
    pl.semaphore_wait(barrier, chips)

    def spread_copy(slot, buffer, source, target):
        return pltpu.make_async_remote_copy(
            src_ref=buffer.at[core, source],
            dst_ref=buffer.at[core, source],
            send_sem=send_ici.at[slot, target],
            recv_sem=recv_ici.at[slot, source],
            device_id=(grp, target * 2 + core),
            device_id_type=LOGICAL,
        )

    def core_copy(slot, buffer, block, side):
        return pltpu.make_async_remote_copy(
            src_ref=buffer.at[side, block],
            dst_ref=buffer.at[side, block],
            send_sem=send_core.at[slot, block],
            recv_sem=recv_core.at[slot, block],
            device_id=partner,
            device_id_type=LOGICAL,
        )

    def spread_start(slot, buffer):
        def body(k, carry):
            spread_copy(slot, buffer, chip, peer(k)).start()
            return carry

        lax.fori_loop(1, chips, body, 0)
        core_copy(slot, buffer, chip, core).start()

    def spread_forward(slot, buffer):
        def body(k, carry):
            j = peer(chips - k)
            spread_copy(slot, buffer, j, j).wait_recv()
            core_copy(slot, buffer, j, core).start()
            return carry

        lax.fori_loop(1, chips, body, 0)

    def spread_finish(slot, buffer):
        def body(k, carry):
            j = peer(chips - k)
            core_copy(slot, buffer, j, other).wait_recv()
            return carry

        lax.fori_loop(0, chips, body, 0)

    def spread_drain(slot, buffer):
        def body(k, carry):
            spread_copy(slot, buffer, chip, peer(k)).wait_send()
            return carry

        def body_core(k, carry):
            core_copy(slot, buffer, peer(k), core).wait_send()
            return carry

        lax.fori_loop(1, chips, body, 0)
        lax.fori_loop(0, chips, body_core, 0)

    spread_start(0, latents)
    spread_start(1, grads)

    embedded = dot_nn(grid_ref[...], embed_ref[...])
    embedded = (embedded * (0.5 * jnp.tanh(0.5 * embedded) + 0.5)).astype(BF16)
    table[...] = dot_nn(embedded, sendw_ref[...]).astype(BF16)
    spread_forward(0, latents)

    per_chunk = CHUNK // LANES

    def pick_senders(step, carry):
        for b in range(per_chunk):
            ids = sender_ref[pl.ds(step * per_chunk + b, 1), :]
            picks[b * LANES : (b + 1) * LANES, :] = selector(ids, picks.shape[1])
        rows = pl.ds(pl.multiple_of(step * CHUNK, CHUNK), CHUNK)
        picked[rows, :] = dot_nn(picks[...], table[...])
        return carry

    lax.fori_loop(0, sub_rows // per_chunk, pick_senders, 0)

    spread_finish(0, latents)
    rtable[...] = dot_nn(latents[...].reshape(nodes, width), recvw_ref[...]).astype(BF16)
    acc[...] = jnp.zeros_like(acc)
    spread_forward(1, grads)

    def sum_edges(step, carry):
        row_parts = []
        for b in range(per_chunk):
            ids = receiver_ref[pl.ds(step * per_chunk + b, 1), :]
            owner = lax.shift_right_logical(ids, shift)
            place = (owner & 1) * half + lax.shift_right_logical(owner, 1) * owned + (ids & (owned - 1))
            rpicks[b * LANES : (b + 1) * LANES, :] = selector(place, nodes)
            row_parts.append(place)
        places = jnp.concatenate(row_parts, axis=1)
        rows = pl.ds(pl.multiple_of(step * CHUNK, CHUNK), CHUNK)
        preact = picked[rows, :] + dot_nn(rpicks[...], rtable[...])
        gates = 0.5 * jnp.tanh(0.5 * preact) + 0.5
        hidden = preact * gates
        slope = gates + hidden * (1.0 - gates)
        position = lax.broadcasted_iota(jnp.int32, (nodes, CHUNK), 0)
        spreader = jnp.where(position == places, 1.0, 0.0).astype(BF16)
        acc[0] += dot_nn(spreader, hidden.astype(BF16)).reshape(2, chips, owned, width)
        acc[1] += dot_nn(spreader, slope.astype(BF16)).reshape(2, chips, owned, width)
        return carry

    lax.fori_loop(0, sub_rows // per_chunk, sum_edges, 0)

    def pair_copy(kind):
        return pltpu.make_async_remote_copy(
            src_ref=outgoing.at[kind],
            dst_ref=pair_in.at[kind],
            send_sem=pair_send.at[kind],
            recv_sem=pair_recv.at[kind],
            device_id=partner,
            device_id_type=LOGICAL,
        )

    def peer_copy(kind, block, source, target):
        return pltpu.make_async_remote_copy(
            src_ref=chip_sum.at[kind, block],
            dst_ref=peer_in.at[kind, source],
            send_sem=peer_send.at[kind, target],
            recv_sem=peer_recv.at[kind, source],
            device_id=(grp, target * 2 + core),
            device_id_type=LOGICAL,
        )

    for kind in range(2):
        outgoing[kind] = acc[kind, other].astype(BF16)
        pair_copy(kind).start()
    for kind in range(2):
        pair_copy(kind).wait_recv()
        total = acc[kind, core] + pair_in[kind].astype(F32)
        acc[kind, core] = total
        chip_sum[kind] = total.astype(BF16)

        def send(k, carry, kind=kind):
            j = peer(k)
            peer_copy(kind, j, chip, j).start()
            return carry

        lax.fori_loop(1, chips, send, 0)

    def collect(kind):
        def body(k, total):
            j = peer(chips - k)
            peer_copy(kind, j, j, j).wait_recv()
            return total + peer_in[kind, j].astype(F32)

        return lax.fori_loop(1, chips, body, acc[kind, core, chip])

    def normalise(rows, upstream):
        summed = dot_nn(rows, messw_ref[...])
        inverse = lax.rsqrt(jnp.mean(summed * summed, axis=-1, keepdims=True) + 1e-05)
        normed = summed * inverse
        dnorm = upstream.astype(F32) * gain_ref[...]
        agg = (inverse * (dnorm - normed * jnp.mean(dnorm * normed, axis=-1, keepdims=True))).astype(BF16)
        return normed, agg

    own_hidden = collect(0).astype(BF16)
    hsums[core, chip] = own_hidden
    spread_start(2, hsums)
    normed, agg = normalise(own_hidden, grad_ref[...])
    update_ref[...] = (latent_ref[...].astype(F32) + normed * gain_ref[...]).astype(BF16)
    hidden_grad = dot_nt(agg, messw_ref[...])
    spread_forward(2, hsums)
    recv_grad = (hidden_grad * collect(1)).astype(BF16)
    meshgrad_ref[...] = (grad_ref[...].astype(F32) + dot_nt(recv_grad, recvw_ref[...])).astype(BF16)
    spread_finish(1, grads)
    spread_finish(2, hsums)
    every = hsums[...].reshape(nodes, width)
    _, all_agg = normalise(every, grads[...].reshape(nodes, width))
    weight_ref[...] = dot_tn(every, all_agg) * (1.0 / math.sqrt(edge_total))

    spread_drain(0, latents)
    spread_drain(1, grads)
    spread_drain(2, hsums)
    for kind in range(2):
        pair_copy(kind).wait_send()

        def drain(k, carry, kind=kind):
            j = peer(k)
            peer_copy(kind, j, chip, j).wait_send()
            return carry

        lax.fori_loop(1, chips, drain, 0)


def shards(
    grid_inputs,
    mesh_latent,
    sender_ids,
    receiver_ids,
    embed_weight,
    sender_weight,
    receiver_weight,
    message_weight,
    norm_gain,
    out_grad,
):
    n = lax.axis_size("node")
    chips = n // 2
    owned, width = mesh_latent.shape
    edges = sender_ids.shape[0]
    senders = grid_inputs.shape[0]
    half = chips * owned
    nodes = 2 * half
    vmem = pl.BlockSpec(memory_space=pltpu.VMEM)
    dma = pltpu.SemaphoreType.DMA
    return pl.pallas_call(
        functools.partial(kernel, chips, edges * n),
        out_shape=(
            jax.ShapeDtypeStruct((owned, width), BF16),
            jax.ShapeDtypeStruct((owned, width), BF16),
            jax.ShapeDtypeStruct((width, width), F32),
        ),
        in_specs=[vmem] * 10,
        out_specs=(vmem, vmem, vmem),
        scratch_shapes=[
            pltpu.VMEM((2, chips, owned, width), BF16),
            pltpu.VMEM((2, chips, owned, width), BF16),
            pltpu.VMEM((2, chips, owned, width), BF16),
            pltpu.VMEM((senders, width), BF16),
            pltpu.VMEM((nodes, width), BF16),
            pltpu.VMEM((edges, width), F32),
            pltpu.VMEM((CHUNK, senders), BF16),
            pltpu.VMEM((CHUNK, nodes), BF16),
            pltpu.VMEM((2, 2, chips, owned, width), F32),
            pltpu.VMEM((2, chips, owned, width), BF16),
            pltpu.VMEM((2, chips, owned, width), BF16),
            pltpu.VMEM((2, chips, owned, width), BF16),
            pltpu.VMEM((2, chips, owned, width), BF16),
            dma((3, chips)),
            dma((3, chips)),
            dma((3, chips)),
            dma((3, chips)),
            dma((2,)),
            dma((2,)),
            dma((2, chips)),
            dma((2, chips)),
        ],
        compiler_params=pltpu.CompilerParams(
            collective_id=0, has_side_effects=True, vmem_limit_bytes=56 * 1024 * 1024
        ),
    )(
        grid_inputs,
        mesh_latent,
        sender_ids.reshape(edges // LANES, LANES),
        receiver_ids.reshape(edges // LANES, LANES),
        embed_weight,
        sender_weight,
        receiver_weight,
        message_weight,
        norm_gain.reshape(1, width),
        out_grad,
    )


def solution(mesh):
    placed = (
        P(("grp", "node"), None),
        P(("grp", "node"), None),
        P(("grp", "node")),
        P(("grp", "node")),
        P(),
        P(),
        P(),
        P(),
        P(),
        P(("grp", "node"), None),
    )
    return jax.shard_map(
        shards,
        mesh=mesh,
        in_specs=placed,
        out_specs=(P(("grp", "node"), None), P(("grp", "node"), None), P("grp", None)),
        check_vma=False,
    )
```

```python
import functools
import math

import jax
import jax.numpy as jnp
from jax import lax
from jax.experimental import pallas as pl
from jax.experimental.pallas import tpu as pltpu
from jax.sharding import PartitionSpec as P

LOGICAL = pl.DeviceIdType.MESH
F32 = jnp.float32
BF16 = jnp.bfloat16
CHUNK = 512
LANES = 128


def dot_nn(a, b):
    return jnp.dot(a, b, preferred_element_type=F32)


def dot_nt(a, b):
    return lax.dot_general(a, b, (((1,), (1,)), ((), ())), preferred_element_type=F32)


def dot_tn(a, b):
    return lax.dot_general(a, b, (((0,), (0,)), ((), ())), preferred_element_type=F32)


def selector(ids_row, columns):
    column = jnp.broadcast_to(ids_row, (LANES, LANES)).T
    lane = lax.broadcasted_iota(jnp.int32, (LANES, LANES), 1)
    parts = [
        jnp.where(column == lane + start, 1.0, 0.0).astype(BF16)
        for start in range(0, columns, LANES)
    ]
    return jnp.concatenate(parts, axis=1)


def kernel(
    chips,
    grid_hbm,
    latent_ref,
    sender_hbm,
    receiver_hbm,
    embed_hbm,
    sendw_hbm,
    recvw_hbm,
    messw_hbm,
    gain_ref,
    grad_ref,
    update_ref,
    meshgrad_ref,
    hidden_ref,
    agg_ref,
    grid_ref,
    sender_ref,
    receiver_ref,
    embed_ref,
    sendw_ref,
    recvw_ref,
    messw_ref,
    latents,
    grads,
    hsums,
    table,
    rtable,
    picked,
    picks,
    rpicks,
    spreader,
    terms,
    acc,
    outgoing,
    pair_in,
    peer_out,
    peer_in,
    load_sem,
    send_ici,
    recv_ici,
    send_core,
    recv_core,
    pair_send,
    pair_recv,
    sum_send,
    sum_recv,
):
    grp = lax.axis_index("grp")
    me = lax.axis_index("node")
    chip = me // 2
    core = me % 2
    other = 1 - core
    owned, width = latent_ref.shape
    half = chips * owned
    nodes = 2 * half
    edges = terms.shape[1]
    shift = owned.bit_length() - 1

    def at(place, c):
        return (grp, place * 2 + c)

    partner = at(chip, other)

    def loop(low, body):
        def step(k, carry):
            body(lax.rem(chip + k, chips))
            return carry

        lax.fori_loop(low, chips, step, 0)

    barrier = pltpu.get_barrier_semaphore()

    def greet(target):
        pl.semaphore_signal(barrier, inc=1, device_id=target, device_id_type=LOGICAL)

    loop(1, lambda j: greet(at(j, core)))
    greet(partner)

    loads = [
        pltpu.make_async_copy(source, target, load_sem.at[i])
        for i, (source, target) in enumerate(
            (
                (embed_hbm, embed_ref),
                (grid_hbm, grid_ref),
                (sendw_hbm, sendw_ref),
                (sender_hbm, sender_ref),
                (receiver_hbm, receiver_ref),
                (recvw_hbm, recvw_ref),
                (messw_hbm, messw_ref),
            )
        )
    ]
    for load in loads:
        load.start()
    latents[core, chip] = latent_ref[...]
    grads[core, chip] = grad_ref[...]

    def chip_copy(slot, buffer, source, target):
        block = buffer.at[core, source]
        return pltpu.make_async_remote_copy(
            src_ref=block,
            dst_ref=block,
            send_sem=send_ici.at[slot, target],
            recv_sem=recv_ici.at[slot, source],
            device_id=at(target, core),
            device_id_type=LOGICAL,
        )

    def core_copy(slot, buffer, place, c):
        block = buffer.at[c, place]
        return pltpu.make_async_remote_copy(
            src_ref=block,
            dst_ref=block,
            send_sem=send_core.at[slot, place],
            recv_sem=recv_core.at[slot, place],
            device_id=partner,
            device_id_type=LOGICAL,
        )

    def spread_start(slot, buffer):
        loop(1, lambda j: chip_copy(slot, buffer, chip, j).start())
        core_copy(slot, buffer, chip, core).start()

    def spread_forward(slot, buffer):
        def body(j):
            chip_copy(slot, buffer, j, j).wait_recv()
            core_copy(slot, buffer, j, core).start()

        loop(1, body)

    def spread_finish(slot, buffer):
        loop(0, lambda j: core_copy(slot, buffer, j, other).wait_recv())

    def spread_drain(slot, buffer):
        loop(1, lambda j: chip_copy(slot, buffer, chip, j).wait_send())
        loop(0, lambda j: core_copy(slot, buffer, j, core).wait_send())

    def embed():
        loads[0].wait()
        loads[1].wait()
        embedded = dot_tn(grid_ref[...], embed_ref[...])
        embedded = (embedded * (0.5 * jnp.tanh(0.5 * embedded) + 0.5)).astype(BF16)
        loads[2].wait()
        table[...] = dot_nn(embedded, sendw_ref[...]).astype(BF16)

    pl.semaphore_wait(barrier, chips)
    spread_start(0, latents)
    embed()
    loads[3].wait()
    loads[4].wait()

    per_chunk = CHUNK // LANES

    def pick_senders(step, carry):
        position = lax.broadcasted_iota(jnp.int32, (nodes, LANES), 0)
        for b in range(per_chunk):
            row = pl.ds(step * per_chunk + b, 1)
            picks[b * LANES : (b + 1) * LANES, :] = selector(sender_ref[row, :], picks.shape[1])
            ids = receiver_ref[row, :]
            owner = lax.shift_right_logical(ids, shift)
            place = (owner & 1) * half + lax.shift_right_logical(owner, 1) * owned + (ids & (owned - 1))
            start = pl.multiple_of(step * CHUNK + b * LANES, LANES)
            rpicks[pl.ds(start, LANES), :] = selector(place, nodes)
            spreader[:, pl.ds(start, LANES)] = jnp.where(position == place, 1.0, 0.0).astype(BF16)
        rows = pl.ds(pl.multiple_of(step * CHUNK, CHUNK), CHUNK)
        picked[rows, :] = dot_nn(picks[...], table[...])
        return carry

    chunks = edges // CHUNK
    lax.fori_loop(0, chunks, pick_senders, 0)
    for load in loads[5:]:
        load.wait()
    spread_forward(0, latents)
    spread_start(1, grads)
    spread_finish(0, latents)
    rtable[...] = dot_nn(latents[...].reshape(nodes, width), recvw_ref[...]).astype(BF16)

    def read_edges(step, carry):
        rows = pl.ds(pl.multiple_of(step * CHUNK, CHUNK), CHUNK)
        preact = picked[rows, :] + dot_nn(rpicks[rows, :], rtable[...])
        gates = 0.5 * jnp.tanh(0.5 * preact) + 0.5
        hidden = preact * gates
        terms[0, rows, :] = hidden.astype(BF16)
        terms[1, rows, :] = (gates + hidden * (1.0 - gates)).astype(BF16)
        return carry

    lax.fori_loop(0, chunks, read_edges, 0)

    def pair_copy(kind):
        return pltpu.make_async_remote_copy(
            src_ref=outgoing.at[kind],
            dst_ref=pair_in.at[kind],
            send_sem=pair_send.at[kind],
            recv_sem=pair_recv.at[kind],
            device_id=partner,
            device_id_type=LOGICAL,
        )

    def sum_copy(kind, block, source, target):
        return pltpu.make_async_remote_copy(
            src_ref=peer_out.at[kind, block],
            dst_ref=peer_in.at[kind, source],
            send_sem=sum_send.at[kind, target],
            recv_sem=sum_recv.at[kind, source],
            device_id=at(target, core),
            device_id_type=LOGICAL,
        )

    def sums(kind, c):
        rows = spreader[pl.ds(pl.multiple_of(c * half, half), half), :]
        return dot_nn(rows, terms[kind])

    def pair_start(kind):
        outgoing[kind] = sums(kind, other).astype(BF16).reshape(chips, owned, width)
        pair_copy(kind).start()

    def own_sums(kind):
        acc[kind] = sums(kind, core).reshape(chips, owned, width)

    def sum_start(kind):
        pair_copy(kind).wait_recv()
        mine = acc[kind] + pair_in[kind].astype(F32)
        acc[kind] = mine
        peer_out[kind] = mine.astype(BF16)
        loop(1, lambda j: sum_copy(kind, j, chip, j).start())

    def collect(kind):
        def body(k, total):
            j = lax.rem(chip + k, chips)
            sum_copy(kind, j, j, j).wait_recv()
            return total + peer_in[kind, j].astype(F32)

        return lax.fori_loop(1, chips, body, acc[kind, chip])

    def normalise(rows, upstream):
        summed = dot_nn(rows, messw_ref[...])
        inverse = lax.rsqrt(jnp.mean(summed * summed, axis=-1, keepdims=True) + 1e-05)
        normed = summed * inverse
        dnorm = upstream.astype(F32) * gain_ref[...]
        agg = (inverse * (dnorm - normed * jnp.mean(dnorm * normed, axis=-1, keepdims=True))).astype(BF16)
        return normed, agg

    pair_start(0)
    own_sums(0)
    sum_start(0)
    pair_start(1)
    own_sums(1)
    sum_start(1)
    spread_forward(1, grads)
    own_hidden = collect(0).astype(BF16)
    hsums[core, chip] = own_hidden
    spread_start(2, hsums)
    normed, agg = normalise(own_hidden, grad_ref[...])
    update_ref[...] = (latent_ref[...].astype(F32) + normed * gain_ref[...]).astype(BF16)
    hidden_grad = dot_nt(agg, messw_ref[...])
    spread_forward(2, hsums)
    recv_grad = (hidden_grad * collect(1)).astype(BF16)
    meshgrad_ref[...] = (grad_ref[...].astype(F32) + dot_nt(recv_grad, recvw_ref[...])).astype(BF16)
    spread_finish(1, grads)
    spread_finish(2, hsums)
    every = hsums[...].reshape(nodes, width)
    hidden_ref[...] = every
    _, all_agg = normalise(every, grads[...].reshape(nodes, width))
    agg_ref[...] = all_agg

    spread_drain(0, latents)
    spread_drain(1, grads)
    spread_drain(2, hsums)
    for kind in range(2):
        pair_copy(kind).wait_send()
        loop(1, lambda j, kind=kind: sum_copy(kind, j, chip, j).wait_send())


def finish(scale, update_in, meshgrad_in, hidden_ref, agg_ref, update_ref, meshgrad_ref, weight_ref):
    update_ref[...] = update_in[...]
    meshgrad_ref[...] = meshgrad_in[...]
    weight_ref[...] = dot_tn(hidden_ref[...], agg_ref[...]) * scale


def shards(
    grid_inputs,
    mesh_latent,
    sender_ids,
    receiver_ids,
    embed_weight,
    sender_weight,
    receiver_weight,
    message_weight,
    norm_gain,
    out_grad,
):
    n = lax.axis_size("node")
    chips = n // 2
    owned, width = mesh_latent.shape
    edges = sender_ids.shape[0]
    senders, channels = grid_inputs.shape
    nodes = n * owned
    vmem = pl.BlockSpec(memory_space=pltpu.VMEM)
    hbm = pl.BlockSpec(memory_space=pl.ANY)
    dma = pltpu.SemaphoreType.DMA
    id_rows = (edges // LANES, LANES)
    blocks = (2, chips, owned, width)
    row = jax.ShapeDtypeStruct((owned, width), BF16)
    every = jax.ShapeDtypeStruct((nodes, width), BF16)
    update, mesh_grad, hidden, agg = pl.pallas_call(
        functools.partial(kernel, chips),
        out_shape=(row, row, every, every),
        in_specs=[hbm, vmem, hbm, hbm, hbm, hbm, hbm, hbm, vmem, vmem],
        out_specs=(vmem, vmem, vmem, vmem),
        scratch_shapes=[
            pltpu.VMEM((channels, senders), BF16),
            pltpu.VMEM(id_rows, jnp.int32),
            pltpu.VMEM(id_rows, jnp.int32),
            pltpu.VMEM(embed_weight.shape, BF16),
            pltpu.VMEM((width, width), BF16),
            pltpu.VMEM((width, width), BF16),
            pltpu.VMEM((width, width), BF16),
            pltpu.VMEM(blocks, BF16),
            pltpu.VMEM(blocks, BF16),
            pltpu.VMEM(blocks, BF16),
            pltpu.VMEM((senders, width), BF16),
            pltpu.VMEM((nodes, width), BF16),
            pltpu.VMEM((edges, width), F32),
            pltpu.VMEM((CHUNK, senders), BF16),
            pltpu.VMEM((edges, nodes), BF16),
            pltpu.VMEM((nodes, edges), BF16),
            pltpu.VMEM((2, edges, width), BF16),
            pltpu.VMEM(blocks, F32),
            pltpu.VMEM(blocks, BF16),
            pltpu.VMEM(blocks, BF16),
            pltpu.VMEM(blocks, BF16),
            pltpu.VMEM(blocks, BF16),
            dma((7,)),
            dma((3, chips)),
            dma((3, chips)),
            dma((3, chips)),
            dma((3, chips)),
            dma((2,)),
            dma((2,)),
            dma((2, chips)),
            dma((2, chips)),
        ],
        compiler_params=pltpu.CompilerParams(
            collective_id=0, has_side_effects=True, vmem_limit_bytes=58 * 1024 * 1024
        ),
    )(
        grid_inputs.T,
        mesh_latent,
        sender_ids.reshape(id_rows),
        receiver_ids.reshape(id_rows),
        embed_weight,
        sender_weight,
        receiver_weight,
        message_weight,
        norm_gain.reshape(1, width),
        out_grad,
    )
    return pl.pallas_call(
        functools.partial(finish, 1.0 / math.sqrt(edges * n)),
        out_shape=(row, row, jax.ShapeDtypeStruct((width, width), F32)),
        in_specs=[vmem] * 4,
        out_specs=(vmem, vmem, vmem),
    )(update, mesh_grad, hidden, agg)


def solution(mesh):
    placed = (
        P(("grp", "node"), None),
        P(("grp", "node"), None),
        P(("grp", "node")),
        P(("grp", "node")),
        P(),
        P(),
        P(),
        P(),
        P(),
        P(("grp", "node"), None),
    )
    return jax.shard_map(
        shards,
        mesh=mesh,
        in_specs=placed,
        out_specs=(P(("grp", "node"), None), P(("grp", "node"), None), P("grp", None)),
        check_vma=False,
    )
```

```python
import functools
import math

import jax
import jax.numpy as jnp
from jax import lax
from jax.experimental import pallas as pl
from jax.experimental.pallas import tpu as pltpu
from jax.sharding import PartitionSpec as P

LOGICAL = pl.DeviceIdType.MESH
F32 = jnp.float32
BF16 = jnp.bfloat16
CHUNK = 512
LANES = 128


def dot_nn(a, b):
    return jnp.dot(a, b, preferred_element_type=F32)


def dot_nt(a, b):
    return lax.dot_general(a, b, (((1,), (1,)), ((), ())), preferred_element_type=F32)


def dot_tn(a, b):
    return lax.dot_general(a, b, (((0,), (0,)), ((), ())), preferred_element_type=F32)


def selector(ids_row, columns):
    column = jnp.broadcast_to(ids_row, (LANES, LANES)).T
    lane = lax.broadcasted_iota(jnp.int32, (LANES, LANES), 1)
    parts = [
        jnp.where(column == lane + start, 1.0, 0.0).astype(BF16)
        for start in range(0, columns, LANES)
    ]
    return jnp.concatenate(parts, axis=1)


def kernel(
    chips,
    grid_hbm,
    latent_hbm,
    sender_hbm,
    receiver_hbm,
    embed_hbm,
    sendw_hbm,
    recvw_hbm,
    messw_hbm,
    gain_hbm,
    grad_hbm,
    update_ref,
    meshgrad_ref,
    hidden_ref,
    agg_ref,
    grid_ref,
    sender_ref,
    receiver_ref,
    embed_ref,
    sendw_ref,
    recvw_ref,
    messw_ref,
    gain_ref,
    latents,
    grads,
    hsums,
    table,
    rtable,
    picked,
    picks,
    rpicks,
    spreader,
    terms,
    acc,
    outgoing,
    pair_in,
    peer_out,
    peer_in,
    load_sem,
    send_ici,
    recv_ici,
    send_core,
    recv_core,
    pair_send,
    pair_recv,
    sum_send,
    sum_recv,
):
    grp = lax.axis_index("grp")
    me = lax.axis_index("node")
    chip = me // 2
    core = me % 2
    other = 1 - core
    owned, width = latent_hbm.shape
    half = chips * owned
    nodes = 2 * half
    edges = terms.shape[1]
    shift = owned.bit_length() - 1

    def at(place, c):
        return (grp, place * 2 + c)

    partner = at(chip, other)

    def loop(low, body):
        def step(k, carry):
            body(lax.rem(chip + k, chips))
            return carry

        lax.fori_loop(low, chips, step, 0)

    barrier = pltpu.get_barrier_semaphore()

    def greet(target):
        pl.semaphore_signal(barrier, inc=1, device_id=target, device_id_type=LOGICAL)

    loop(1, lambda j: greet(at(j, core)))
    greet(partner)

    loads = [
        pltpu.make_async_copy(source, target, load_sem.at[i])
        for i, (source, target) in enumerate(
            (
                (latent_hbm, latents.at[core, chip]),
                (grad_hbm, grads.at[core, chip]),
                (embed_hbm, embed_ref),
                (grid_hbm, grid_ref),
                (sendw_hbm, sendw_ref),
                (sender_hbm, sender_ref),
                (receiver_hbm, receiver_ref),
                (recvw_hbm, recvw_ref),
                (messw_hbm, messw_ref),
                (gain_hbm, gain_ref),
            )
        )
    ]
    for load in loads:
        load.start()
    loads[0].wait()
    loads[1].wait()

    def chip_copy(slot, buffer, source, target):
        block = buffer.at[core, source]
        return pltpu.make_async_remote_copy(
            src_ref=block,
            dst_ref=block,
            send_sem=send_ici.at[slot, target],
            recv_sem=recv_ici.at[slot, source],
            device_id=at(target, core),
            device_id_type=LOGICAL,
        )

    def core_copy(slot, buffer, place, c):
        block = buffer.at[c, place]
        return pltpu.make_async_remote_copy(
            src_ref=block,
            dst_ref=block,
            send_sem=send_core.at[slot, place],
            recv_sem=recv_core.at[slot, place],
            device_id=partner,
            device_id_type=LOGICAL,
        )

    def spread_start(slot, buffer):
        loop(1, lambda j: chip_copy(slot, buffer, chip, j).start())
        core_copy(slot, buffer, chip, core).start()

    def spread_forward(slot, buffer):
        def body(j):
            chip_copy(slot, buffer, j, j).wait_recv()
            core_copy(slot, buffer, j, core).start()

        loop(1, body)

    def spread_finish(slot, buffer):
        loop(0, lambda j: core_copy(slot, buffer, j, other).wait_recv())

    def spread_drain(slot, buffer):
        loop(1, lambda j: chip_copy(slot, buffer, chip, j).wait_send())
        loop(0, lambda j: core_copy(slot, buffer, j, core).wait_send())

    def embed():
        loads[2].wait()
        loads[3].wait()
        embedded = dot_tn(grid_ref[...], embed_ref[...])
        embedded = (embedded * (0.5 * jnp.tanh(0.5 * embedded) + 0.5)).astype(BF16)
        loads[4].wait()
        table[...] = dot_nn(embedded, sendw_ref[...]).astype(BF16)

    pl.semaphore_wait(barrier, chips)
    spread_start(0, latents)
    embed()
    loads[5].wait()
    loads[6].wait()

    per_chunk = CHUNK // LANES

    def pick_senders(step, carry):
        position = lax.broadcasted_iota(jnp.int32, (nodes, LANES), 0)
        for b in range(per_chunk):
            row = pl.ds(step * per_chunk + b, 1)
            picks[b * LANES : (b + 1) * LANES, :] = selector(sender_ref[row, :], picks.shape[1])
            ids = receiver_ref[row, :]
            owner = lax.shift_right_logical(ids, shift)
            place = (owner & 1) * half + lax.shift_right_logical(owner, 1) * owned + (ids & (owned - 1))
            start = pl.multiple_of(step * CHUNK + b * LANES, LANES)
            rpicks[pl.ds(start, LANES), :] = selector(place, nodes)
            spreader[:, pl.ds(start, LANES)] = jnp.where(position == place, 1.0, 0.0).astype(BF16)
        rows = pl.ds(pl.multiple_of(step * CHUNK, CHUNK), CHUNK)
        picked[rows, :] = dot_nn(picks[...], table[...])
        return carry

    chunks = edges // CHUNK
    lax.fori_loop(0, chunks, pick_senders, 0)
    for load in loads[7:]:
        load.wait()
    spread_forward(0, latents)
    spread_start(1, grads)
    spread_finish(0, latents)
    rtable[...] = dot_nn(latents[...].reshape(nodes, width), recvw_ref[...]).astype(BF16)

    def read_edges(step, carry):
        rows = pl.ds(pl.multiple_of(step * CHUNK, CHUNK), CHUNK)
        preact = picked[rows, :] + dot_nn(rpicks[rows, :], rtable[...])
        gates = 0.5 * jnp.tanh(0.5 * preact) + 0.5
        hidden = preact * gates
        terms[0, rows, :] = hidden.astype(BF16)
        terms[1, rows, :] = (gates + hidden * (1.0 - gates)).astype(BF16)
        return carry

    lax.fori_loop(0, chunks, read_edges, 0)

    def pair_copy(kind):
        return pltpu.make_async_remote_copy(
            src_ref=outgoing.at[kind],
            dst_ref=pair_in.at[kind],
            send_sem=pair_send.at[kind],
            recv_sem=pair_recv.at[kind],
            device_id=partner,
            device_id_type=LOGICAL,
        )

    def sum_copy(kind, block, source, target):
        return pltpu.make_async_remote_copy(
            src_ref=peer_out.at[kind, block],
            dst_ref=peer_in.at[kind, source],
            send_sem=sum_send.at[kind, target],
            recv_sem=sum_recv.at[kind, source],
            device_id=at(target, core),
            device_id_type=LOGICAL,
        )

    def sums(kind, c):
        rows = spreader[pl.ds(pl.multiple_of(c * half, half), half), :]
        return dot_nn(rows, terms[kind])

    def pair_start(kind):
        outgoing[kind] = sums(kind, other).astype(BF16).reshape(chips, owned, width)
        pair_copy(kind).start()

    def own_sums(kind):
        acc[kind] = sums(kind, core).reshape(chips, owned, width)

    def sum_start(kind):
        pair_copy(kind).wait_recv()
        mine = acc[kind] + pair_in[kind].astype(F32)
        acc[kind] = mine
        peer_out[kind] = mine.astype(BF16)
        loop(1, lambda j: sum_copy(kind, j, chip, j).start())

    def collect(kind):
        def body(k, total):
            j = lax.rem(chip + k, chips)
            sum_copy(kind, j, j, j).wait_recv()
            return total + peer_in[kind, j].astype(F32)

        return lax.fori_loop(1, chips, body, acc[kind, chip])

    def normalise(rows, upstream):
        summed = dot_nn(rows, messw_ref[...])
        inverse = lax.rsqrt(jnp.mean(summed * summed, axis=-1, keepdims=True) + 1e-05)
        normed = summed * inverse
        dnorm = upstream.astype(F32) * gain_ref[...]
        agg = (inverse * (dnorm - normed * jnp.mean(dnorm * normed, axis=-1, keepdims=True))).astype(BF16)
        return normed, agg

    pair_start(0)
    own_sums(0)
    sum_start(0)
    pair_start(1)
    own_sums(1)
    sum_start(1)
    spread_forward(1, grads)
    own_hidden = collect(0).astype(BF16)
    hsums[core, chip] = own_hidden
    spread_start(2, hsums)
    normed, agg = normalise(own_hidden, grads[core, chip])
    update_ref[...] = (latents[core, chip].astype(F32) + normed * gain_ref[...]).astype(BF16)
    hidden_grad = dot_nt(agg, messw_ref[...])
    spread_forward(2, hsums)
    recv_grad = (hidden_grad * collect(1)).astype(BF16)
    meshgrad_ref[...] = (grads[core, chip].astype(F32) + dot_nt(recv_grad, recvw_ref[...])).astype(BF16)
    spread_finish(1, grads)
    spread_finish(2, hsums)
    every = hsums[...].reshape(nodes, width)
    hidden_ref[...] = every
    _, all_agg = normalise(every, grads[...].reshape(nodes, width))
    agg_ref[...] = all_agg

    spread_drain(0, latents)
    spread_drain(1, grads)
    spread_drain(2, hsums)
    for kind in range(2):
        pair_copy(kind).wait_send()
        loop(1, lambda j, kind=kind: sum_copy(kind, j, chip, j).wait_send())


def finish(scale, update_in, meshgrad_in, hidden_ref, agg_ref, update_ref, meshgrad_ref, weight_ref):
    update_ref[...] = update_in[...]
    meshgrad_ref[...] = meshgrad_in[...]
    weight_ref[...] = dot_tn(hidden_ref[...], agg_ref[...]) * scale


def shards(
    grid_inputs,
    mesh_latent,
    sender_ids,
    receiver_ids,
    embed_weight,
    sender_weight,
    receiver_weight,
    message_weight,
    norm_gain,
    out_grad,
):
    n = lax.axis_size("node")
    chips = n // 2
    owned, width = mesh_latent.shape
    edges = sender_ids.shape[0]
    senders, channels = grid_inputs.shape
    nodes = n * owned
    vmem = pl.BlockSpec(memory_space=pltpu.VMEM)
    hbm = pl.BlockSpec(memory_space=pl.ANY)
    dma = pltpu.SemaphoreType.DMA
    id_rows = (edges // LANES, LANES)
    blocks = (2, chips, owned, width)
    row = jax.ShapeDtypeStruct((owned, width), BF16)
    every = jax.ShapeDtypeStruct((nodes, width), BF16)
    update, mesh_grad, hidden, agg = pl.pallas_call(
        functools.partial(kernel, chips),
        out_shape=(row, row, every, every),
        in_specs=[hbm] * 10,
        out_specs=(vmem, vmem, vmem, vmem),
        scratch_shapes=[
            pltpu.VMEM((channels, senders), BF16),
            pltpu.VMEM(id_rows, jnp.int32),
            pltpu.VMEM(id_rows, jnp.int32),
            pltpu.VMEM(embed_weight.shape, BF16),
            pltpu.VMEM((width, width), BF16),
            pltpu.VMEM((width, width), BF16),
            pltpu.VMEM((width, width), BF16),
            pltpu.VMEM((1, width), F32),
            pltpu.VMEM(blocks, BF16),
            pltpu.VMEM(blocks, BF16),
            pltpu.VMEM(blocks, BF16),
            pltpu.VMEM((senders, width), BF16),
            pltpu.VMEM((nodes, width), BF16),
            pltpu.VMEM((edges, width), F32),
            pltpu.VMEM((CHUNK, senders), BF16),
            pltpu.VMEM((edges, nodes), BF16),
            pltpu.VMEM((nodes, edges), BF16),
            pltpu.VMEM((2, edges, width), BF16),
            pltpu.VMEM(blocks, F32),
            pltpu.VMEM(blocks, BF16),
            pltpu.VMEM(blocks, BF16),
            pltpu.VMEM(blocks, BF16),
            pltpu.VMEM(blocks, BF16),
            dma((10,)),
            dma((3, chips)),
            dma((3, chips)),
            dma((3, chips)),
            dma((3, chips)),
            dma((2,)),
            dma((2,)),
            dma((2, chips)),
            dma((2, chips)),
        ],
        compiler_params=pltpu.CompilerParams(
            collective_id=0, has_side_effects=True, vmem_limit_bytes=61 * 1024 * 1024
        ),
    )(
        grid_inputs.T,
        mesh_latent,
        sender_ids.reshape(id_rows),
        receiver_ids.reshape(id_rows),
        embed_weight,
        sender_weight,
        receiver_weight,
        message_weight,
        norm_gain.reshape(1, width),
        out_grad,
    )
    return pl.pallas_call(
        functools.partial(finish, 1.0 / math.sqrt(edges * n)),
        out_shape=(row, row, jax.ShapeDtypeStruct((width, width), F32)),
        in_specs=[vmem] * 4,
        out_specs=(vmem, vmem, vmem),
    )(update, mesh_grad, hidden, agg)


def solution(mesh):
    placed = (
        P(("grp", "node"), None),
        P(("grp", "node"), None),
        P(("grp", "node")),
        P(("grp", "node")),
        P(),
        P(),
        P(),
        P(),
        P(),
        P(("grp", "node"), None),
    )
    return jax.shard_map(
        shards,
        mesh=mesh,
        in_specs=placed,
        out_specs=(P(("grp", "node"), None), P(("grp", "node"), None), P("grp", None)),
        check_vma=False,
    )
```

```python
import functools
import math

import jax
import jax.numpy as jnp
from jax import lax
from jax.experimental import pallas as pl
from jax.experimental.pallas import tpu as pltpu
from jax.sharding import PartitionSpec as P

LOGICAL = pl.DeviceIdType.MESH
F32 = jnp.float32
BF16 = jnp.bfloat16
CHUNK = 1024
LANES = 128


def dot_nn(a, b):
    return jnp.dot(a, b, preferred_element_type=F32)


def dot_nt(a, b):
    return lax.dot_general(a, b, (((1,), (1,)), ((), ())), preferred_element_type=F32)


def dot_tn(a, b):
    return lax.dot_general(a, b, (((0,), (0,)), ((), ())), preferred_element_type=F32)


def selector(ids_row, columns):
    column = jnp.broadcast_to(ids_row, (LANES, LANES)).T
    lane = lax.broadcasted_iota(jnp.int32, (LANES, LANES), 1)
    parts = [
        jnp.where(column == lane + start, 1.0, 0.0).astype(BF16)
        for start in range(0, columns, LANES)
    ]
    return jnp.concatenate(parts, axis=1)


def kernel(
    chips,
    grid_hbm,
    latent_hbm,
    sender_hbm,
    receiver_hbm,
    embed_hbm,
    sendw_hbm,
    recvw_hbm,
    messw_hbm,
    gain_hbm,
    grad_hbm,
    update_ref,
    meshgrad_ref,
    hidden_ref,
    agg_ref,
    grid_ref,
    sender_ref,
    receiver_ref,
    embed_ref,
    sendw_ref,
    recvw_ref,
    messw_ref,
    gain_ref,
    latents,
    grads,
    hsums,
    table,
    rtable,
    picked,
    picks,
    rpicks,
    spreader,
    terms,
    acc,
    outgoing,
    pair_in,
    peer_out,
    peer_in,
    load_sem,
    send_ici,
    recv_ici,
    send_core,
    recv_core,
    pair_send,
    pair_recv,
    sum_send,
    sum_recv,
):
    grp = lax.axis_index("grp")
    me = lax.axis_index("node")
    chip = me // 2
    core = me % 2
    other = 1 - core
    owned, width = latent_hbm.shape
    half = chips * owned
    nodes = 2 * half
    edges = terms.shape[1]
    shift = owned.bit_length() - 1

    def at(place, c):
        return (grp, place * 2 + c)

    partner = at(chip, other)

    def loop(low, body):
        def step(k, carry):
            body(lax.rem(chip + k, chips))
            return carry

        lax.fori_loop(low, chips, step, 0)

    barrier = pltpu.get_barrier_semaphore()

    def greet(target):
        pl.semaphore_signal(barrier, inc=1, device_id=target, device_id_type=LOGICAL)

    loop(1, lambda j: greet(at(j, core)))
    greet(partner)

    loads = [
        pltpu.make_async_copy(source, target, load_sem.at[i])
        for i, (source, target) in enumerate(
            (
                (latent_hbm, latents.at[core, chip]),
                (grad_hbm, grads.at[core, chip]),
                (embed_hbm, embed_ref),
                (grid_hbm, grid_ref),
                (sendw_hbm, sendw_ref),
                (sender_hbm, sender_ref),
                (receiver_hbm, receiver_ref),
                (recvw_hbm, recvw_ref),
                (messw_hbm, messw_ref),
                (gain_hbm, gain_ref),
            )
        )
    ]
    for load in loads:
        load.start()
    loads[0].wait()
    loads[1].wait()

    def chip_copy(slot, buffer, source, target):
        block = buffer.at[core, source]
        return pltpu.make_async_remote_copy(
            src_ref=block,
            dst_ref=block,
            send_sem=send_ici.at[slot, target],
            recv_sem=recv_ici.at[slot, source],
            device_id=at(target, core),
            device_id_type=LOGICAL,
        )

    def core_copy(slot, buffer, place, c):
        block = buffer.at[c, place]
        return pltpu.make_async_remote_copy(
            src_ref=block,
            dst_ref=block,
            send_sem=send_core.at[slot, place],
            recv_sem=recv_core.at[slot, place],
            device_id=partner,
            device_id_type=LOGICAL,
        )

    def spread_start(slot, buffer):
        loop(1, lambda j: chip_copy(slot, buffer, chip, j).start())
        core_copy(slot, buffer, chip, core).start()

    def spread_forward(slot, buffer):
        def body(j):
            chip_copy(slot, buffer, j, j).wait_recv()
            core_copy(slot, buffer, j, core).start()

        loop(1, body)

    def spread_finish(slot, buffer):
        loop(0, lambda j: core_copy(slot, buffer, j, other).wait_recv())

    def spread_drain(slot, buffer):
        loop(1, lambda j: chip_copy(slot, buffer, chip, j).wait_send())
        loop(0, lambda j: core_copy(slot, buffer, j, core).wait_send())

    def embed():
        loads[2].wait()
        loads[3].wait()
        embedded = dot_tn(grid_ref[...], embed_ref[...])
        embedded = (embedded * (0.5 * jnp.tanh(0.5 * embedded) + 0.5)).astype(BF16)
        loads[4].wait()
        table[...] = dot_nn(embedded, sendw_ref[...]).astype(BF16)

    pl.semaphore_wait(barrier, chips)
    spread_start(0, latents)
    embed()
    loads[5].wait()
    loads[6].wait()

    per_chunk = CHUNK // LANES

    def pick_senders(step, carry):
        position = lax.broadcasted_iota(jnp.int32, (nodes, LANES), 0)
        for b in range(per_chunk):
            row = pl.ds(step * per_chunk + b, 1)
            picks[b * LANES : (b + 1) * LANES, :] = selector(sender_ref[row, :], picks.shape[1])
            ids = receiver_ref[row, :]
            owner = lax.shift_right_logical(ids, shift)
            place = (owner & 1) * half + lax.shift_right_logical(owner, 1) * owned + (ids & (owned - 1))
            start = pl.multiple_of(step * CHUNK + b * LANES, LANES)
            rpicks[pl.ds(start, LANES), :] = selector(place, nodes)
            spreader[:, pl.ds(start, LANES)] = jnp.where(position == place, 1.0, 0.0).astype(BF16)
        rows = pl.ds(pl.multiple_of(step * CHUNK, CHUNK), CHUNK)
        picked[rows, :] = dot_nn(picks[...], table[...])
        return carry

    chunks = edges // CHUNK
    lax.fori_loop(0, chunks, pick_senders, 0)
    for load in loads[7:]:
        load.wait()
    spread_forward(0, latents)
    spread_start(1, grads)
    spread_finish(0, latents)
    rtable[...] = dot_nn(latents[...].reshape(nodes, width), recvw_ref[...]).astype(BF16)

    def read_edges(step, carry):
        rows = pl.ds(pl.multiple_of(step * CHUNK, CHUNK), CHUNK)
        preact = picked[rows, :] + dot_nn(rpicks[rows, :], rtable[...])
        gates = 0.5 * jnp.tanh(0.5 * preact) + 0.5
        hidden = preact * gates
        terms[0, rows, :] = hidden.astype(BF16)
        terms[1, rows, :] = (gates + hidden * (1.0 - gates)).astype(BF16)
        return carry

    lax.fori_loop(0, chunks, read_edges, 0)

    def pair_copy(kind):
        return pltpu.make_async_remote_copy(
            src_ref=outgoing.at[kind],
            dst_ref=pair_in.at[kind],
            send_sem=pair_send.at[kind],
            recv_sem=pair_recv.at[kind],
            device_id=partner,
            device_id_type=LOGICAL,
        )

    def sum_copy(kind, block, source, target):
        return pltpu.make_async_remote_copy(
            src_ref=peer_out.at[kind, block],
            dst_ref=peer_in.at[kind, source],
            send_sem=sum_send.at[kind, target],
            recv_sem=sum_recv.at[kind, source],
            device_id=at(target, core),
            device_id_type=LOGICAL,
        )

    def sums(kind, c):
        rows = spreader[pl.ds(pl.multiple_of(c * half, half), half), :]
        return dot_nn(rows, terms[kind])

    def pair_start(kind):
        outgoing[kind] = sums(kind, other).astype(BF16).reshape(chips, owned, width)
        pair_copy(kind).start()

    def own_sums(kind):
        acc[kind] = sums(kind, core).reshape(chips, owned, width)

    def sum_start(kind):
        pair_copy(kind).wait_recv()
        mine = acc[kind] + pair_in[kind].astype(F32)
        acc[kind] = mine
        peer_out[kind] = mine.astype(BF16)
        loop(1, lambda j: sum_copy(kind, j, chip, j).start())

    def collect(kind):
        def body(k, total):
            j = lax.rem(chip + k, chips)
            sum_copy(kind, j, j, j).wait_recv()
            return total + peer_in[kind, j].astype(F32)

        return lax.fori_loop(1, chips, body, acc[kind, chip])

    def normalise(rows, upstream):
        summed = dot_nn(rows, messw_ref[...])
        inverse = lax.rsqrt(jnp.mean(summed * summed, axis=-1, keepdims=True) + 1e-05)
        normed = summed * inverse
        dnorm = upstream.astype(F32) * gain_ref[...]
        agg = (inverse * (dnorm - normed * jnp.mean(dnorm * normed, axis=-1, keepdims=True))).astype(BF16)
        return normed, agg

    pair_start(0)
    own_sums(0)
    sum_start(0)
    pair_start(1)
    own_sums(1)
    sum_start(1)
    spread_forward(1, grads)
    own_hidden = collect(0).astype(BF16)
    hsums[core, chip] = own_hidden
    spread_start(2, hsums)
    normed, agg = normalise(own_hidden, grads[core, chip])
    update_ref[...] = (latents[core, chip].astype(F32) + normed * gain_ref[...]).astype(BF16)
    hidden_grad = dot_nt(agg, messw_ref[...])
    spread_forward(2, hsums)
    recv_grad = (hidden_grad * collect(1)).astype(BF16)
    meshgrad_ref[...] = (grads[core, chip].astype(F32) + dot_nt(recv_grad, recvw_ref[...])).astype(BF16)
    spread_finish(1, grads)
    spread_finish(2, hsums)
    every = hsums[...].reshape(nodes, width)
    hidden_ref[...] = every
    _, all_agg = normalise(every, grads[...].reshape(nodes, width))
    agg_ref[...] = all_agg

    spread_drain(0, latents)
    spread_drain(1, grads)
    spread_drain(2, hsums)
    for kind in range(2):
        pair_copy(kind).wait_send()
        loop(1, lambda j, kind=kind: sum_copy(kind, j, chip, j).wait_send())


def finish(scale, update_in, meshgrad_in, hidden_ref, agg_ref, update_ref, meshgrad_ref, weight_ref):
    update_ref[...] = update_in[...]
    meshgrad_ref[...] = meshgrad_in[...]
    weight_ref[...] = dot_tn(hidden_ref[...], agg_ref[...]) * scale


def shards(
    grid_inputs,
    mesh_latent,
    sender_ids,
    receiver_ids,
    embed_weight,
    sender_weight,
    receiver_weight,
    message_weight,
    norm_gain,
    out_grad,
):
    n = lax.axis_size("node")
    chips = n // 2
    owned, width = mesh_latent.shape
    edges = sender_ids.shape[0]
    senders, channels = grid_inputs.shape
    nodes = n * owned
    vmem = pl.BlockSpec(memory_space=pltpu.VMEM)
    hbm = pl.BlockSpec(memory_space=pl.ANY)
    dma = pltpu.SemaphoreType.DMA
    id_rows = (edges // LANES, LANES)
    blocks = (2, chips, owned, width)
    row = jax.ShapeDtypeStruct((owned, width), BF16)
    every = jax.ShapeDtypeStruct((nodes, width), BF16)
    update, mesh_grad, hidden, agg = pl.pallas_call(
        functools.partial(kernel, chips),
        out_shape=(row, row, every, every),
        in_specs=[hbm] * 10,
        out_specs=(vmem, vmem, vmem, vmem),
        scratch_shapes=[
            pltpu.VMEM((channels, senders), BF16),
            pltpu.VMEM(id_rows, jnp.int32),
            pltpu.VMEM(id_rows, jnp.int32),
            pltpu.VMEM(embed_weight.shape, BF16),
            pltpu.VMEM((width, width), BF16),
            pltpu.VMEM((width, width), BF16),
            pltpu.VMEM((width, width), BF16),
            pltpu.VMEM((1, width), F32),
            pltpu.VMEM(blocks, BF16),
            pltpu.VMEM(blocks, BF16),
            pltpu.VMEM(blocks, BF16),
            pltpu.VMEM((senders, width), BF16),
            pltpu.VMEM((nodes, width), BF16),
            pltpu.VMEM((edges, width), F32),
            pltpu.VMEM((CHUNK, senders), BF16),
            pltpu.VMEM((edges, nodes), BF16),
            pltpu.VMEM((nodes, edges), BF16),
            pltpu.VMEM((2, edges, width), BF16),
            pltpu.VMEM(blocks, F32),
            pltpu.VMEM(blocks, BF16),
            pltpu.VMEM(blocks, BF16),
            pltpu.VMEM(blocks, BF16),
            pltpu.VMEM(blocks, BF16),
            dma((10,)),
            dma((3, chips)),
            dma((3, chips)),
            dma((3, chips)),
            dma((3, chips)),
            dma((2,)),
            dma((2,)),
            dma((2, chips)),
            dma((2, chips)),
        ],
        compiler_params=pltpu.CompilerParams(
            collective_id=0, has_side_effects=True, vmem_limit_bytes=61 * 1024 * 1024
        ),
    )(
        grid_inputs.T,
        mesh_latent,
        sender_ids.reshape(id_rows),
        receiver_ids.reshape(id_rows),
        embed_weight,
        sender_weight,
        receiver_weight,
        message_weight,
        norm_gain.reshape(1, width),
        out_grad,
    )
    return pl.pallas_call(
        functools.partial(finish, 1.0 / math.sqrt(edges * n)),
        out_shape=(row, row, jax.ShapeDtypeStruct((width, width), F32)),
        in_specs=[vmem] * 4,
        out_specs=(vmem, vmem, vmem),
    )(update, mesh_grad, hidden, agg)


def solution(mesh):
    placed = (
        P(("grp", "node"), None),
        P(("grp", "node"), None),
        P(("grp", "node")),
        P(("grp", "node")),
        P(),
        P(),
        P(),
        P(),
        P(),
        P(("grp", "node"), None),
    )
    return jax.shard_map(
        shards,
        mesh=mesh,
        in_specs=placed,
        out_specs=(P(("grp", "node"), None), P(("grp", "node"), None), P("grp", None)),
        check_vma=False,
    )
```
